256 devices in a mesh: dp: 128 (over z, x, y), mp: 2 (over core).
Axes of the slice: x: 4, y: 4, z: 8, core: 2. Of those that a mesh axis runs over, the one named last changes fastest.
Arguments:
- gradient: float32 [131072, 512], P('dp', 'mp'), may hold values from -12 to 12
- moment: float32 [131072, 512], P('dp', 'mp'), may hold values from 0.01 to 1
- left_stat: float32 [128, 1024, 1024], P('dp', 'mp'), may hold values from -1 to 3
- right_stat: float32 [128, 512, 512], P('dp', 'mp'), may hold values from -1 to 3
- left_root: bfloat16 [128, 1024, 1024], P('dp'), may hold values from -1 to 5
- right_root: bfloat16 [128, 512, 512], P('dp', None, 'mp'), may hold values from -1 to 5
- seg_block: int32 [131072], P('dp'), may hold values from 0 to 127, as said below
- seg_row: int32 [131072], P('dp'), may hold values from 0 to 1023, as said below
- owner_table: int32 [128], replicated, may hold values from 0 to 127, as said below
Outputs:
- update: bfloat16 [131072, 512], P('dp', 'mp')
- moment_new: float32 [131072, 512], P('dp', 'mp')
- left_new: float32 [128, 1024, 1024], P('dp', 'mp')
- right_new: float32 [128, 512, 512], P('dp', 'mp')
The draws below stay inside these ranges and needn't reach their ends.
Inputs may be any that keep to these rules, and one draw needn't show every extreme that they name: `seg_block`: over all devices, every block's rows 0 to 1023 each appear exactly once. The rows of one device hold at most 12 rows of one block, and some device holds exactly 12 rows of some block in every draw. Every row of one device belongs to a block whose owner differs from the device by the same amount for as many rows on every device; each owner receives 1024 rows. `seg_row`: together with seg_block, names each block row exactly once. `owner_table`: each device owns exactly one block.
All inputs are finite; a program needn't handle non-finite values.
Results may differ from the reference program's by a relative error of at most 0.0058.
Values may be sent and summed in bfloat16 or wider, within the bound.
No kernel may reach another device: no remote copies, remote signals or barrier semaphores. Data moves between devices by JAX's collectives and lax.ppermute only.
A program may use at most 64 MiB of HBM per device.

```python
import math
import jax
import jax.numpy as jnp
from jax import lax

BROWS = 1024
BCOLS = 512
BLOCKS = 128
N_DP = 128


def layout(key):
    owners_count = N_DP
    typical = BROWS // owners_count
    half_count = owners_count // 2
    owner_perm = jax.random.permutation(jax.random.fold_in(key, 11), owners_count).astype(jnp.int32)
    spread = jax.random.randint(jax.random.fold_in(key, 12), (half_count,), 0, typical // 2 + 1)
    sign_values = jax.random.randint(jax.random.fold_in(key, 13), (half_count,), 0, 2) * 2 - 1
    peak_index = jax.random.randint(jax.random.fold_in(key, 14), (), 1, half_count)
    positions = jnp.arange(half_count)
    spread = jnp.where(positions == peak_index, typical // 2, spread)
    sign_values = jnp.where(positions == peak_index, 1, sign_values)
    offsets = spread * sign_values
    counts = jnp.concatenate([typical + offsets, typical - offsets])
    bounds = jnp.cumsum(counts)
    slot_ids = jnp.arange(BROWS)
    offset_of = jnp.sum((slot_ids[:, None] >= bounds[None, :-1]).astype(jnp.int32), axis=1)
    row_perm = jax.random.permutation(jax.random.fold_in(key, 15), BROWS).astype(jnp.int32)
    device_keys = jax.random.split(jax.random.fold_in(key, 16), owners_count)
    slot_perm = jax.vmap(lambda sub_key: jax.random.permutation(sub_key, BROWS))(device_keys)
    device_ids = jnp.arange(owners_count)[:, None]
    owners = (device_ids + offset_of[slot_perm]) % owners_count
    inverse = jnp.argsort(owner_perm).astype(jnp.int32)
    blocks = inverse[owners]
    seg_rows = row_perm[slot_perm]
    return (blocks.reshape(-1).astype(jnp.int32), seg_rows.reshape(-1).astype(jnp.int32), owner_perm)


def symmetric(key, total_blocks, matrix_size, lowest, highest, spread):
    diag_key, jitter_key = jax.random.split(key)
    diagonal = jnp.exp(jax.random.uniform(diag_key, (total_blocks, matrix_size), minval=math.log(lowest), maxval=math.log(highest)))
    jitter = jax.random.normal(jitter_key, (total_blocks, matrix_size, matrix_size)) * (spread / math.sqrt(matrix_size))
    mirrored = 0.5 * (jitter + jnp.swapaxes(jitter, 1, 2))
    identity = jnp.eye(matrix_size, dtype=jnp.float32)
    return mirrored + identity[None] * diagonal[:, :, None]


def draw_seg_block(key, part):
    return layout(key)[0]


def draw_seg_row(key, part):
    return layout(key)[1]


def draw_owner_table(key, part):
    return layout(key)[2]


def draw_gradient(key, part):
    key = jax.random.fold_in(key, 21)
    total_rows = BLOCKS * BROWS
    noise_key = jax.random.fold_in(key, 1)
    row_key = jax.random.fold_in(key, 2)
    col_key = jax.random.fold_in(key, 3)
    values = jax.random.normal(noise_key, (total_rows, BCOLS))
    lowest = 10.0 ** (-0.5)
    highest = 10.0 ** 0.5
    row_scale = jnp.exp(jax.random.uniform(row_key, (total_rows, 1), minval=math.log(lowest), maxval=math.log(highest)))
    col_scale = jnp.exp(jax.random.uniform(col_key, (1, BCOLS), minval=math.log(lowest), maxval=math.log(highest)))
    device_pos = (jnp.arange(total_rows) // BROWS).astype(jnp.float32)
    trend = 3.0 ** (device_pos / max(BLOCKS - 1, 1))
    return (values * row_scale * col_scale * trend[:, None] * (0.4 / math.sqrt(BCOLS))).astype(jnp.float32)


def draw_left_stat(key, part):
    key = jax.random.fold_in(key, 31)
    return symmetric(key, BLOCKS, BROWS, 0.2, 2.0, 0.3)


def draw_right_stat(key, part):
    key = jax.random.fold_in(key, 32)
    return symmetric(key, BLOCKS, BCOLS, 0.2, 2.0, 0.3)


def draw_left_root(key, part):
    key = jax.random.fold_in(key, 33)
    return symmetric(key, BLOCKS, BROWS, 0.5, 2.0, 0.5).astype(jnp.bfloat16)


def draw_right_root(key, part):
    key = jax.random.fold_in(key, 34)
    return symmetric(key, BLOCKS, BCOLS, 0.5, 2.0, 0.5).astype(jnp.bfloat16)


def block_scale(key, extent, cuts, low, high):
    gain, own = 1.0, jax.random.fold_in(key, 6)
    for dim, shards_of in cuts:
        heights = jnp.exp(jax.random.uniform(jax.random.fold_in(own, dim), (shards_of,), jnp.float32, low / len(cuts), high / len(cuts)))
        gain = gain * jnp.repeat(heights, extent[dim] // shards_of).reshape([-1 if axis == dim else 1 for axis in range(len(extent))])
    return gain


def setup_inputs(seed: int = 0) -> dict:
    splits = jax.random.split(jax.random.key(seed), 10)
    gradient = draw_gradient(jax.random.fold_in(splits[9], 71), 0)
    moment = jnp.clip(jnp.exp(math.log(1.0) - 4.6051702 * jax.random.uniform(splits[1], (BLOCKS * BROWS, BCOLS), jnp.float32) ** block_scale(splits[1], (BLOCKS * BROWS, BCOLS), ((0, 128), (1, 2)), -0.2, 0.2)), 0.01, 1.0)
    left_stat = draw_left_stat(jax.random.fold_in(splits[9], 71), 0)
    right_stat = draw_right_stat(jax.random.fold_in(splits[9], 71), 0)
    left_root = draw_left_root(jax.random.fold_in(splits[9], 71), 0)
    right_root = draw_right_root(jax.random.fold_in(splits[9], 71), 0)
    seg_block = draw_seg_block(jax.random.fold_in(splits[9], 71), 0)
    seg_row = draw_seg_row(jax.random.fold_in(splits[9], 71), 0)
    owner_table = draw_owner_table(jax.random.fold_in(splits[9], 71), 0)
    return dict(gradient=gradient, moment=moment, left_stat=left_stat, right_stat=right_stat, left_root=left_root, right_root=right_root, seg_block=seg_block, seg_row=seg_row, owner_table=owner_table)


GRAM_DECAY = 0.95
MOMENT_DECAY = 0.99
ADAM_EPS = 1e-08
GRAFT_EPS = 1e-06

def reference(gradient, moment, left_stat, right_stat, left_root, right_root, seg_block, seg_row, owner_table):
    moment_new = MOMENT_DECAY * moment + (1.0 - MOMENT_DECAY) * gradient * gradient
    adam_step = gradient / (jnp.sqrt(moment_new) + ADAM_EPS)
    seg_sq = lax.optimization_barrier(jnp.sum(adam_step * adam_step, axis=1))
    seg_owner = owner_table[seg_block].astype(jnp.int32)
    row_index = seg_row.astype(jnp.int32)
    adam_sq = jax.ops.segment_sum(seg_sq, seg_owner, num_segments=BLOCKS)
    tiles = jnp.zeros((BLOCKS, BROWS, BCOLS), gradient.dtype).at[seg_owner, row_index].set(gradient)

    def per_owner(operands):
        tile, left_prev, right_prev, left_inv, right_inv, adam_total = operands
        left_next = GRAM_DECAY * left_prev + jnp.dot(tile, tile.T, precision=lax.Precision.HIGHEST, preferred_element_type=jnp.float32)
        right_next = GRAM_DECAY * right_prev + jnp.dot(tile.T, tile, precision=lax.Precision.HIGHEST, preferred_element_type=jnp.float32)
        mixed = jnp.dot(tile.astype(jnp.bfloat16), right_inv, preferred_element_type=jnp.float32).astype(jnp.bfloat16)
        precond = jnp.dot(left_inv, mixed, preferred_element_type=jnp.float32)
        graft_scale = jnp.sqrt(adam_total) / (jnp.sqrt(jnp.sum(precond * precond)) + GRAFT_EPS)
        return (left_next, right_next, (precond * graft_scale).astype(jnp.bfloat16))
    left_new, right_new, grafted = lax.map(per_owner, (tiles, left_stat, right_stat, left_root, right_root, adam_sq))
    update = grafted[seg_owner, row_index]
    return (update, moment_new, left_new, right_new)
```

```python
import functools
import jax
import jax.numpy as jnp
from jax import lax
from jax.experimental import pallas as pl
from jax.experimental.pallas import tpu as pltpu
from jax.sharding import PartitionSpec as P

GRAM_DECAY = 0.95
MOMENT_DECAY = 0.99
ADAM_EPS = 1e-08
GRAFT_EPS = 1e-06

CAP = 12
OUT = CAP + 1
LANES = 128
BF = jnp.bfloat16
F32 = jnp.float32
VMEM_LIMIT = 32 * 1024 * 1024
CHUNKS = 3
VMEM = pl.BlockSpec(memory_space=pltpu.VMEM)
SMEM = pl.BlockSpec(memory_space=pltpu.SMEM)
HBM = pl.BlockSpec(memory_space=pltpu.HBM)
shape = jax.ShapeDtypeStruct


def iota(shape, dim):
    return lax.broadcasted_iota(jnp.int32, shape, dim)


def dot(a, b):
    return jnp.dot(a, b, preferred_element_type=F32)


def dot_nt(a, b):
    return lax.dot_general(a, b, (((1,), (1,)), ((), ())), preferred_element_type=F32)


def onehot(mask):
    return jnp.where(mask, 1.0, 0.0).astype(BF)


def split3(x):
    hi = x.astype(BF)
    rest = x - hi.astype(F32)
    mid = rest.astype(BF)
    lo = (rest - mid.astype(F32)).astype(BF)
    return hi, mid, lo


def keep(x):
    return pltpu.with_memory_space_constraint(x, pltpu.HBM)


def call(kernel, out_shape, in_specs, out_specs=None, scratch=(), flops=0, nbytes=0):
    return pl.pallas_call(
        kernel,
        out_shape=out_shape,
        in_specs=in_specs,
        out_specs=out_specs if out_specs else jax.tree.map(lambda _: VMEM, out_shape),
        scratch_shapes=list(scratch),
        compiler_params=pltpu.CompilerParams(vmem_limit_bytes=VMEM_LIMIT),
        cost_estimate=pl.CostEstimate(flops=flops, bytes_accessed=nbytes, transcendentals=0),
    )


def ranks(dest):
    rows = dest.shape[1]
    step = 256 if rows % 256 == 0 else rows
    before = onehot(iota((step, step), 0) < iota((step, step), 1))
    found, parts = 0.0, []
    for start in range(0, rows, step):
        part = dest[:, start : start + step]
        parts.append(dot(part, before) + found)
        found = found + jnp.sum(part.astype(F32), axis=1, keepdims=True)
    return jnp.concatenate(parts, axis=1)


def pack_kernel(
    n, grad_hbm, moment_hbm, block_hbm, row_hbm, owner_hbm, send_ref, place_ref, new_hbm,
    grad_ref, moment_ref, block_ref, row_ref, owner_ref, scr, sems,
):
    rows = grad_ref.shape[0]
    pairs = (
        (block_hbm, block_ref), (owner_hbm, owner_ref), (row_hbm, row_ref), (grad_hbm, grad_ref),
        (moment_hbm, moment_ref),
    )
    copies = [pltpu.make_async_copy(a, b, sems.at[i]) for i, (a, b) in enumerate(pairs)]
    for copy in copies:
        copy.start()
    for copy in copies[:3]:
        copy.wait()
    block = block_ref[...]
    blocks = onehot(iota((n, rows), 0) == block)
    owner = jnp.broadcast_to(owner_ref[...], (16, n)).astype(F32).astype(BF)
    target = dot(owner, blocks)[0:1].astype(jnp.int32)
    mine = iota((n, rows), 0) == target
    dest = onehot(mine)
    slot = jnp.sum(jnp.where(mine, ranks(dest), 0.0), axis=0, keepdims=True).astype(jnp.int32)
    place_ref[...] = CAP * target + slot
    code = OUT * target + slot
    lane = iota((LANES, rows), 0)
    position = row_ref[...] + 1
    spread = jnp.where(lane == slot, position // 32, 0) + jnp.where(lane == slot + 16, position % 32, 0)
    meta = dot_nt(dest, spread.astype(F32).astype(BF))
    copies[3].wait()
    copies[4].wait()

    grad = grad_ref[...]
    square = grad * grad
    moment = MOMENT_DECAY * moment_ref[...] + (1.0 - MOMENT_DECAY) * square
    moment_ref[...] = moment
    store = pltpu.make_async_copy(moment_ref, new_hbm, sems.at[5])
    store.start()
    denom = jnp.sqrt(moment) + ADAM_EPS
    step = grad / denom
    step_sq = step * step
    half = step_sq[:, :LANES] + step_sq[:, LANES:]
    hi, mid, lo = split3(half)
    adam = jnp.sum(dot(dest, hi) + dot(dest, mid) + dot(dest, lo), axis=1, keepdims=True)
    a_hi, a_mid, a_lo = split3(adam)
    col = iota((n, LANES), 1)
    meta = jnp.where(col == 32, a_hi.astype(F32), meta)
    meta = jnp.where(col == 33, a_mid.astype(F32), meta)
    meta = jnp.where(col == 34, a_lo.astype(F32), meta)

    placed = dot(onehot(iota((OUT * n, rows), 0) == code), grad.astype(BF))
    scr[pl.ds(0, OUT * n, stride=2), :] = placed[:, :LANES]
    scr[pl.ds(1, OUT * n, stride=2), :] = placed[:, LANES:]
    scr[pl.ds(2 * CAP, n, stride=2 * OUT), :] = meta
    send_ref[...] = scr[...].astype(BF)
    store.wait()


def pack(n, gradient, moment, block, row, owner):
    rows, width = gradient.shape
    return call(
        functools.partial(pack_kernel, n),
        (shape((2 * OUT * n, LANES), BF), shape((1, rows), jnp.int32), shape((rows, width), F32)),
        [HBM] * 5,
        (VMEM, VMEM, HBM),
        [
            pltpu.VMEM((rows, width), F32),
            pltpu.VMEM((rows, width), F32),
            pltpu.VMEM((1, rows), jnp.int32),
            pltpu.VMEM((1, rows), jnp.int32),
            pltpu.VMEM((1, n), jnp.int32),
            pltpu.VMEM((2 * OUT * n, LANES), F32),
            pltpu.SemaphoreType.DMA((6,)),
        ],
        flops=2 * OUT * n * rows * width, nbytes=4 * 2**20,
    )(*[keep(x) for x in (gradient, moment, block, row, owner)])


def column_halves(scr, start, slots):
    left = scr[pl.ds(2 * start, slots, stride=2), :].astype(BF)
    right = scr[pl.ds(2 * start + 1, slots, stride=2), :].astype(BF)
    return jnp.concatenate([left, right], axis=1)


def tile_kernel(n, got_ref, left_hbm, tile_ref, adam_ref, meta_ref, left_ref, scr, sem):
    load = pltpu.make_async_copy(left_hbm.at[pl.ds(0, left_ref.shape[0])], left_ref, sem)
    load.start()
    rows = tile_ref.shape[0]
    scr[...] = got_ref[...].astype(F32)
    meta = scr[pl.ds(2 * CAP, n, stride=2 * OUT), :]
    meta_ref[...] = meta
    col = iota((n, LANES), 1)
    adam = jnp.sum(jnp.where((col >= 32) & (col < 35), meta, 0.0), axis=(0, 1), keepdims=True)
    adam_ref[...] = jnp.broadcast_to(adam, adam_ref.shape)
    source = iota((n, OUT * n), 0)
    slots = iota((n, OUT * n), 1)
    expand = onehot((slots >= OUT * source) & (slots < OUT * source + OUT))
    by_slot = dot(meta.T.astype(BF), expand)
    position = 32.0 * by_slot[0:16] + by_slot[16:32]
    which = iota((16, OUT * n), 1) % OUT
    position = jnp.sum(
        jnp.where(iota((16, OUT * n), 0) == which, position, 0.0), axis=0, keepdims=True
    ).astype(jnp.int32)
    order = onehot(iota((rows, OUT * n), 0) + 1 == position)
    tile_ref[...] = dot(order, column_halves(scr, 0, OUT * n)).astype(BF)
    load.wait()


def tile(n, rows, got, left):
    return call(
        functools.partial(tile_kernel, n),
        (
            shape((rows, 2 * LANES), BF), shape((8, LANES), F32), shape((n, LANES), F32),
            shape((rows // 2, rows), BF),
        ),
        [VMEM, HBM],
        scratch=[pltpu.VMEM((2 * OUT * n, LANES), F32), pltpu.SemaphoreType.DMA],
        flops=2 * OUT * n * rows * 2 * LANES, nbytes=3 * 2**20,
    )(got, keep(left))


def return_order_kernel(n, meta_ref, left_hbm, order_ref, left_ref, sem):
    half = left_ref.shape[0]
    load = pltpu.make_async_copy(left_hbm.at[pl.ds(half, half)], left_ref, sem)
    load.start()
    rows = order_ref.shape[1]
    slots = iota((CAP * n, n), 0)
    source = iota((CAP * n, n), 1)
    expand = onehot((slots >= CAP * source) & (slots < CAP * source + CAP))
    meta = meta_ref[...]
    meta = jnp.where(iota((n, LANES), 1) < 16, 32.0 * meta, meta).astype(BF)
    by_slot = dot(expand, meta)
    which = iota((CAP * n, LANES), 0) % CAP
    lane = iota((CAP * n, LANES), 1)
    chosen = jnp.where((lane == which) | (lane == which + 16), by_slot, 0.0).astype(BF)
    position = dot(chosen, jnp.ones((LANES, LANES), BF)).astype(jnp.int32)
    lane = lane + 1
    for j in range(0, rows, LANES):
        order_ref[:, j : j + LANES] = onehot(position == lane + j)
    load.wait()


def return_order(n, rows, meta, left):
    return call(
        functools.partial(return_order_kernel, n),
        (shape((CAP * n, rows), BF), shape((rows // 2, rows), BF)),
        [VMEM, HBM],
        scratch=[pltpu.SemaphoreType.DMA],
        flops=4 * CAP * n * n * LANES, nbytes=4 * 2**20,
    )(meta, keep(left))


def precond_kernel(
    n, core_ref, own_ref, other_ref, adam_own_ref, adam_other_ref, order_ref, root_own_ref,
    root_other_ref, left_top_ref, left_bottom_ref, back_hbm, scr, back_ref, sems,
):
    rows, width = own_ref.shape
    core = core_ref[0]
    own_rows = pl.ds(pl.multiple_of(core * width, width), width)
    other_rows = pl.ds(pl.multiple_of((1 - core) * width, width), width)
    own, other = own_ref[...], other_ref[...]
    mixed_own = dot(own, root_own_ref[own_rows, :]) + dot(other, root_own_ref[other_rows, :])
    mixed_other = dot(own, root_other_ref[own_rows, :]) + dot(other, root_other_ref[other_rows, :])
    mixed_own, mixed_other = mixed_own.astype(BF), mixed_other.astype(BF)
    parts, total = [], 0.0
    for left_ref in (left_top_ref, left_bottom_ref):
        for start in range(0, rows // 2, rows // 4):
            left = left_ref[start : start + rows // 4, :]
            part, other_part = dot(left, mixed_own), dot(left, mixed_other)
            squares = part * part + other_part * other_part
            total = total + jnp.sum(squares.reshape(rows // 32, 8, width), axis=0)
            parts.append(part)
    total = jnp.sum(total, axis=(0, 1), keepdims=True)
    adam = adam_own_ref[0:1, 0:1] + adam_other_ref[0:1, 0:1]
    scale = jnp.sqrt(adam) / (jnp.sqrt(total) + GRAFT_EPS)
    grafted = jnp.concatenate([(part * scale).astype(BF) for part in parts], axis=0)
    part = CAP * n // CHUNKS
    stores = []
    for i in range(CHUNKS):
        chunk = pl.ds(2 * part * i, 2 * part)
        placed = dot(order_ref[part * i : part * (i + 1), :], grafted)
        scr[pl.ds(2 * part * i, part, stride=2), :] = placed[:, :LANES]
        scr[pl.ds(2 * part * i + 1, part, stride=2), :] = placed[:, LANES:]
        back_ref[chunk, :] = scr[chunk, :].astype(BF)
        store = pltpu.make_async_copy(back_ref.at[chunk], back_hbm.at[chunk], sems.at[i])
        store.start()
        stores.append(store)
    for store in stores:
        store.wait()


def precond(
    n, core, own, other, adam_own, adam_other, order, root_own, root_other, left_top, left_bottom
):
    rows, width = own.shape
    return call(
        functools.partial(precond_kernel, n),
        shape((2 * CAP * n, LANES), BF),
        [SMEM] + [VMEM] * 9,
        HBM,
        scratch=[
            pltpu.VMEM((2 * CAP * n, LANES), F32),
            pltpu.VMEM((2 * CAP * n, LANES), BF),
            pltpu.SemaphoreType.DMA((CHUNKS,)),
        ],
        flops=8 * rows * rows * width, nbytes=5 * 2**20,
    )(core, own, other, adam_own, adam_other, order, root_own, root_other, left_top, left_bottom)


def flat_order_kernel(n, place_ref, after_ref, order_ref):
    del after_ref
    rows = order_ref.shape[0]
    place = jnp.broadcast_to(place_ref[...].astype(F32), (LANES, rows)).T.astype(jnp.int32)
    lane = iota((rows, LANES), 1)
    for j in range(0, CAP * n, LANES):
        order_ref[:, j : j + LANES] = onehot(place == lane + j)


def flat_order(n, place, after):
    rows = place.shape[1]
    return call(
        functools.partial(flat_order_kernel, n),
        shape((rows, CAP * n), BF),
        [VMEM, pl.BlockSpec(memory_space=pl.ANY)],
        flops=0, nbytes=3 * 2**20,
    )(place, after)


def unpack_kernel(n, back_hbm, order_ref, update_hbm, back_ref, scr, update_ref, sems):
    rows = update_ref.shape[0]
    part = CAP * n // CHUNKS
    loads = []
    for i in range(CHUNKS):
        chunk = pl.ds(2 * part * i, 2 * part)
        loads.append(pltpu.make_async_copy(back_hbm.at[chunk], back_ref.at[chunk], sems.at[i]))
        loads[i].start()
    halves = [pl.ds(i * (rows // 2), rows // 2) for i in range(2)]
    sums = [0.0, 0.0]
    for i in range(CHUNKS):
        chunk = pl.ds(2 * part * i, 2 * part)
        loads[i].wait()
        scr[chunk, :] = back_ref[chunk, :].astype(F32)
        came = column_halves(scr, part * i, part)
        for j, half in enumerate(halves):
            sums[j] = sums[j] + dot(order_ref[half, part * i : part * (i + 1)], came)
            if i == CHUNKS - 1:
                update_ref[half, :] = sums[j].astype(BF)
                store = pltpu.make_async_copy(update_ref.at[half], update_hbm.at[half], sems.at[CHUNKS + j])
                store.start()
                loads.append(store)
    for store in loads[CHUNKS:]:
        store.wait()


def unpack(n, back, order):
    rows = order.shape[0]
    return call(
        functools.partial(unpack_kernel, n),
        shape((rows, 2 * LANES), BF),
        [HBM, VMEM],
        HBM,
        scratch=[
            pltpu.VMEM((2 * CAP * n, LANES), BF),
            pltpu.VMEM((2 * CAP * n, LANES), F32),
            pltpu.VMEM((rows, 2 * LANES), BF),
            pltpu.SemaphoreType.DMA((CHUNKS + 2,)),
        ],
        flops=2 * CAP * n * rows * 2 * LANES, nbytes=2 * 2**20,
    )(back, order)


def body(
    gradient, moment, left_stat, right_stat, left_root, right_root, seg_block, seg_row, owner_table
):
    n = lax.axis_size("dp")
    rows = gradient.shape[0]
    core = lax.axis_index("mp").astype(jnp.int32)
    swap = [(0, 1), (1, 0)]
    root_own = right_root[0]
    root_other = lax.ppermute(root_own, "mp", swap)

    send, place, moment_new = pack(
        n, gradient, moment, seg_block[None, :], seg_row[None, :], owner_table[None, :]
    )
    send, root_other = lax.optimization_barrier((send, root_other))
    got = lax.all_to_all(send.reshape(n, OUT, 2, LANES), "dp", 0, 0, tiled=True)
    got = got.reshape(2 * OUT * n, LANES)
    tile_own, adam_own, meta, left_top = tile(n, rows, got, left_root[0])
    tile_other = lax.ppermute(tile_own, "mp", swap)
    adam_other = lax.ppermute(adam_own, "mp", swap)
    order, left_bottom = return_order(n, rows, meta, left_root[0])
    back = precond(
        n, core[None], tile_own, tile_other, adam_own, adam_other, order, root_own, root_other,
        left_top, left_bottom,
    )
    returned = lax.all_to_all(back.reshape(n, 2 * CAP, LANES), "dp", 0, 0, tiled=True)

    order = flat_order(n, place, back)
    whole = jnp.where(
        core == 0,
        jnp.concatenate([tile_own, tile_other], axis=1),
        jnp.concatenate([tile_other, tile_own], axis=1),
    )
    stat_rows = left_stat.shape[1]
    own_rows = lax.dynamic_slice_in_dim(whole, core * stat_rows, stat_rows, 0)
    left_new = GRAM_DECAY * left_stat[0] + dot_nt(own_rows, whole)
    right_new = GRAM_DECAY * right_stat[0] + lax.dot_general(
        tile_own, whole, (((0,), (0,)), ((), ())), preferred_element_type=F32
    )
    update = unpack(n, returned.reshape(2 * CAP * n, LANES), order)
    return (update, moment_new, left_new[None], right_new[None])


def solution(mesh):
    in_specs = (
        P("dp", "mp"),
        P("dp", "mp"),
        P("dp", "mp", None),
        P("dp", "mp", None),
        P("dp", None, None),
        P("dp", None, "mp"),
        P("dp"),
        P("dp"),
        P(),
    )
    out_specs = (P("dp", "mp"), P("dp", "mp"), P("dp", "mp", None), P("dp", "mp", None))
    return jax.shard_map(body, mesh=mesh, in_specs=in_specs, out_specs=out_specs, check_vma=False)
```

```python
import functools
import jax
import jax.numpy as jnp
from jax import lax
from jax.experimental import pallas as pl
from jax.experimental.pallas import tpu as pltpu
from jax.sharding import PartitionSpec as P

GRAM_DECAY = 0.95
MOMENT_DECAY = 0.99
ADAM_EPS = 1e-08
GRAFT_EPS = 1e-06

CAP = 12
OUT = CAP + 1
LANES = 128
BF = jnp.bfloat16
F32 = jnp.float32
VMEM_LIMIT = 32 * 1024 * 1024
EXTRA = 16
GROUP = 4
LOADS = 2
CHUNKS = 4
PARTS = 3
VMEM = pl.BlockSpec(memory_space=pltpu.VMEM)
SMEM = pl.BlockSpec(memory_space=pltpu.SMEM)
HBM = pl.BlockSpec(memory_space=pltpu.HBM)
shape = jax.ShapeDtypeStruct


def iota(shape, dim):
    return lax.broadcasted_iota(jnp.int32, shape, dim)


def dot(a, b):
    return jnp.dot(a, b, preferred_element_type=F32)


def dot_nt(a, b):
    return lax.dot_general(a, b, (((1,), (1,)), ((), ())), preferred_element_type=F32)


def onehot(mask):
    return jnp.where(mask, 1.0, 0.0).astype(BF)


def split3(x):
    hi = x.astype(BF)
    rest = x - hi.astype(F32)
    mid = rest.astype(BF)
    lo = (rest - mid.astype(F32)).astype(BF)
    return hi, mid, lo


def keep(x):
    return pltpu.with_memory_space_constraint(x, pltpu.HBM)


def call(kernel, out_shape, in_specs, out_specs=None, scratch=(), flops=0, nbytes=0):
    return pl.pallas_call(
        kernel,
        out_shape=out_shape,
        in_specs=in_specs,
        out_specs=out_specs if out_specs else jax.tree.map(lambda _: VMEM, out_shape),
        scratch_shapes=list(scratch),
        compiler_params=pltpu.CompilerParams(vmem_limit_bytes=VMEM_LIMIT),
        cost_estimate=pl.CostEstimate(flops=flops, bytes_accessed=nbytes, transcendentals=0),
    )


def ranks(dest):
    rows = dest.shape[1]
    step = 256 if rows % 256 == 0 else rows
    before = onehot(iota((step, step), 0) < iota((step, step), 1))
    found, parts = 0.0, []
    for start in range(0, rows, step):
        part = dest[:, start : start + step]
        parts.append(dot(part, before) + found)
        found = found + jnp.sum(part.astype(F32), axis=1, keepdims=True)
    return jnp.concatenate(parts, axis=1)


def next_moment(grad, moment):
    return MOMENT_DECAY * moment + (1.0 - MOMENT_DECAY) * (grad * grad)


def pack_kernel(
    n, grad_hbm, moment_hbm, block_hbm, row_hbm, owner_hbm, send_ref, place_ref, grad_ref,
    moment_ref, block_ref, row_ref, owner_ref, scr, sems,
):
    rows = grad_ref.shape[0]
    pairs = ((block_hbm, block_ref), (owner_hbm, owner_ref), (row_hbm, row_ref))
    copies = [pltpu.make_async_copy(a, b, sems.at[i]) for i, (a, b) in enumerate(pairs)]
    parts = [pl.ds(i * (rows // LOADS), rows // LOADS) for i in range(LOADS)]
    loads = [
        [
            pltpu.make_async_copy(grad_hbm.at[part], grad_ref.at[part], sems.at[3 + 2 * i]),
            pltpu.make_async_copy(moment_hbm.at[part], moment_ref.at[part], sems.at[4 + 2 * i]),
        ]
        for i, part in enumerate(parts)
    ]
    for copy in copies + sum(loads, []):
        copy.start()
    for copy in copies:
        copy.wait()
    block = block_ref[...]
    blocks = onehot(iota((n, rows), 0) == block)
    owner = jnp.broadcast_to(owner_ref[...], (16, n)).astype(F32).astype(BF)
    target = dot(owner, blocks)[0:1].astype(jnp.int32)
    mine = iota((n, rows), 0) == target
    dest = onehot(mine)
    slot = jnp.sum(jnp.where(mine, ranks(dest), 0.0), axis=0, keepdims=True).astype(jnp.int32)
    place_ref[...] = CAP * target + slot
    lane = iota((LANES, rows), 0)
    position = row_ref[...] + 1
    spread = jnp.where(lane == slot, position // 32, 0) + jnp.where(lane == slot + 16, position % 32, 0)
    meta = dot_nt(dest, spread.astype(F32).astype(BF))
    squares, coarse = [], []
    for part, (load_grad, load_moment) in zip(parts, loads):
        load_grad.wait()
        load_moment.wait()
        grad = grad_ref[part, :]
        coarse.append(grad.astype(BF))
        step = grad / (jnp.sqrt(next_moment(grad, moment_ref[part, :])) + ADAM_EPS)
        step_sq = step * step
        half = step_sq[:, :LANES] + step_sq[:, LANES:]
        squares.append(jnp.concatenate(split3(half), axis=1))
    coarse = jnp.concatenate(coarse, axis=0)
    for start in range(0, CAP, GROUP):
        slots = range(start, start + GROUP)
        order = jnp.concatenate([dest * onehot(slot == k) for k in slots], axis=0)
        placed = dot(order, coarse)
        for i, k in enumerate(slots):
            scr[pl.ds(2 * k, n, stride=2 * OUT), :] = placed[n * i : n * (i + 1), :LANES]
            scr[pl.ds(2 * k + 1, n, stride=2 * OUT), :] = placed[n * i : n * (i + 1), LANES:]
    adam = dot(dest, jnp.concatenate(squares, axis=0))
    a_hi, a_mid, a_lo = split3(jnp.sum(adam, axis=1, keepdims=True))
    col = iota((n, LANES), 1)
    meta = jnp.where(col == 32, a_hi.astype(F32), meta)
    meta = jnp.where(col == 33, a_mid.astype(F32), meta)
    meta = jnp.where(col == 34, a_lo.astype(F32), meta)
    scr[pl.ds(2 * CAP, n, stride=2 * OUT), :] = meta
    scr[pl.ds(2 * CAP + 1, n, stride=2 * OUT), :] = jnp.zeros((n, LANES), F32)
    send_ref[...] = scr[...].astype(BF)


def pack(n, gradient, moment, block, row, owner):
    rows, width = gradient.shape
    return call(
        functools.partial(pack_kernel, n),
        (shape((2 * OUT * n, LANES), BF), shape((1, rows), jnp.int32)),
        [HBM] * 5,
        scratch=[
            pltpu.VMEM((rows, width), F32),
            pltpu.VMEM((rows, width), F32),
            pltpu.VMEM((1, rows), jnp.int32),
            pltpu.VMEM((1, rows), jnp.int32),
            pltpu.VMEM((1, n), jnp.int32),
            pltpu.VMEM((2 * OUT * n, LANES), F32),
            pltpu.SemaphoreType.DMA((3 + 2 * LOADS,)),
        ],
        flops=2 * OUT * n * rows * width, nbytes=4 * 2**20,
    )(*[keep(x) for x in (gradient, moment, block, row, owner)])


def column_halves(scr, start, slots):
    left = scr[pl.ds(2 * start, slots, stride=2), :].astype(BF)
    right = scr[pl.ds(2 * start + 1, slots, stride=2), :].astype(BF)
    return jnp.concatenate([left, right], axis=1)


def tile_kernel(
    n, got_ref, root_hbm, tile_ref, meta_ref, root_ref, scr, sem
):
    load = pltpu.make_async_copy(root_hbm, root_ref, sem)
    load.start()
    rows = tile_ref.shape[0] - EXTRA
    scr[...] = got_ref[...].astype(F32)
    meta = scr[pl.ds(2 * CAP, n, stride=2 * OUT), :]
    meta_ref[...] = meta
    col = iota((n, LANES), 1)
    adam = jnp.sum(jnp.where((col >= 32) & (col < 35), meta, 0.0), axis=(0, 1), keepdims=True)
    col = iota((EXTRA, 2 * LANES), 1)
    extra = jnp.zeros((EXTRA, 2 * LANES), F32)
    for i, piece in enumerate(split3(adam)):
        extra = jnp.where(col == i, piece.astype(F32), extra)
    tile_ref[rows:, :] = extra.astype(BF)
    by_slot = meta.T
    position = (32.0 * by_slot[0:16] + by_slot[16:32]).astype(jnp.int32)
    came = []
    for k in range(CAP):
        left = scr[pl.ds(2 * k, n, stride=2 * OUT), :].astype(BF)
        right = scr[pl.ds(2 * k + 1, n, stride=2 * OUT), :].astype(BF)
        came.append(jnp.concatenate([left, right], axis=1))
    came = jnp.concatenate(came, axis=0)
    step = rows // 4
    for start in range(0, rows, step):
        row = iota((step, n), 0) + (start + 1)
        order = [onehot(row == position[k : k + 1]) for k in range(CAP)]
        tile_ref[start : start + step, :] = dot(jnp.concatenate(order, axis=1), came).astype(BF)
    load.wait()


def tile(n, rows, got, root):
    return call(
        functools.partial(tile_kernel, n),
        (
            shape((rows + EXTRA, 2 * LANES), BF), shape((n, LANES), F32), shape(root.shape, BF),
        ),
        [VMEM, HBM],
        scratch=[pltpu.VMEM((2 * OUT * n, LANES), F32), pltpu.SemaphoreType.DMA],
        flops=2 * OUT * n * rows * 2 * LANES, nbytes=3 * 2**20,
    )(got, keep(root))


def return_order_kernel(n, meta_ref, left_hbm, order_ref, left_ref, sem):
    load = pltpu.make_async_copy(left_hbm.at[pl.ds(0, left_ref.shape[0])], left_ref, sem)
    load.start()
    rows = order_ref.shape[1]
    slots = iota((CAP * n, n), 0)
    source = iota((CAP * n, n), 1)
    expand = onehot((slots >= CAP * source) & (slots < CAP * source + CAP))
    meta = meta_ref[...]
    meta = jnp.where(iota((n, LANES), 1) < 16, 32.0 * meta, meta).astype(BF)
    by_slot = dot(expand, meta)
    which = iota((CAP * n, LANES), 0) % CAP
    lane = iota((CAP * n, LANES), 1)
    chosen = jnp.where((lane == which) | (lane == which + 16), by_slot, 0.0).astype(BF)
    position = dot(chosen, jnp.ones((LANES, LANES), BF)).astype(jnp.int32)
    lane = lane + 1
    for j in range(0, rows, LANES):
        order_ref[:, j : j + LANES] = onehot(position == lane + j)
    load.wait()


def return_order(n, rows, meta, left):
    return call(
        functools.partial(return_order_kernel, n),
        (shape((CAP * n, rows), BF), shape((3 * rows // 4, rows), BF)),
        [VMEM, HBM],
        scratch=[pltpu.SemaphoreType.DMA],
        flops=4 * CAP * n * n * LANES, nbytes=4 * 2**20,
    )(meta, keep(left))


def precond_kernel(
    n, core_ref, own_ref, other_ref, order_ref, root_own_ref, root_other_ref, left_ref,
    left_hbm, back_hbm, rest_ref, scr, back_ref, sems,
):
    rows, width = own_ref.shape[0] - EXTRA, own_ref.shape[1]
    quarter = rows // 4
    load = pltpu.make_async_copy(left_hbm.at[pl.ds(3 * quarter, quarter)], rest_ref, sems.at[CHUNKS])
    load.start()
    core = core_ref[0]
    own_rows = pl.ds(pl.multiple_of(core * width, width), width)
    other_rows = pl.ds(pl.multiple_of((1 - core) * width, width), width)
    both = jnp.concatenate([own_ref[:rows, :], other_ref[:rows, :]], axis=1)
    mixed = []
    for root_ref in (root_own_ref, root_other_ref):
        root = jnp.concatenate([root_ref[own_rows, :], root_ref[other_rows, :]], axis=0)
        mixed.append(dot(both, root).astype(BF))
    mixed_own, mixed_other = mixed
    parts, total = [], 0.0
    for i in range(4):
        if i == 3:
            load.wait()
        left = rest_ref[...] if i == 3 else left_ref[quarter * i : quarter * (i + 1), :]
        part, other_part = dot(left, mixed_own), dot(left, mixed_other)
        squares = part * part + other_part * other_part
        total = total + jnp.sum(squares.reshape(quarter // 8, 8, width), axis=0)
        parts.append(part)
    total = jnp.sum(total, axis=(0, 1), keepdims=True)
    extra = own_ref[rows:, :].astype(F32) + other_ref[rows:, :].astype(F32)
    adam = jnp.sum(extra[0:1], axis=(0, 1), keepdims=True)
    scale = jnp.sqrt(adam) / (jnp.sqrt(total) + GRAFT_EPS)
    grafted = jnp.concatenate([(part * scale).astype(BF) for part in parts], axis=0)
    part = CAP * n // CHUNKS
    stores = []
    for i in range(CHUNKS):
        chunk = pl.ds(2 * part * i, 2 * part)
        placed = dot(order_ref[part * i : part * (i + 1), :], grafted)
        scr[pl.ds(2 * part * i, part, stride=2), :] = placed[:, :LANES]
        scr[pl.ds(2 * part * i + 1, part, stride=2), :] = placed[:, LANES:]
        back_ref[chunk, :] = scr[chunk, :].astype(BF)
        store = pltpu.make_async_copy(back_ref.at[chunk], back_hbm.at[chunk], sems.at[i])
        store.start()
        stores.append(store)
    for store in stores:
        store.wait()


def precond(
    n, core, own, other, order, root_own, root_other, left_near, left
):
    rows, width = own.shape[0] - EXTRA, own.shape[1]
    return call(
        functools.partial(precond_kernel, n),
        shape((2 * CAP * n, LANES), BF),
        [SMEM] + [VMEM] * 6 + [HBM],
        HBM,
        scratch=[
            pltpu.VMEM((rows // 4, rows), BF),
            pltpu.VMEM((2 * CAP * n, LANES), F32),
            pltpu.VMEM((2 * CAP * n, LANES), BF),
            pltpu.SemaphoreType.DMA((CHUNKS + 1,)),
        ],
        flops=8 * rows * rows * width, nbytes=5 * 2**20,
    )(core, own, other, order, root_own, root_other, left_near, keep(left))


def beside_kernel(
    n, place_ref, after_ref, grad_hbm, moment_hbm, order_ref, new_hbm, grad_ref, moment_ref, sems
):
    del after_ref
    rows = order_ref.shape[0]
    loads = [
        pltpu.make_async_copy(grad_hbm, grad_ref, sems.at[0]),
        pltpu.make_async_copy(moment_hbm, moment_ref, sems.at[1]),
    ]
    for load in loads:
        load.start()
    place = jnp.broadcast_to(place_ref[...].astype(F32), (LANES, rows)).T.astype(jnp.int32)
    lane = iota((rows, LANES), 1)
    for j in range(0, CAP * n, LANES):
        order_ref[:, j : j + LANES] = onehot(place == lane + j)
    for load in loads:
        load.wait()
    moment_ref[...] = next_moment(grad_ref[...], moment_ref[...])
    store = pltpu.make_async_copy(moment_ref, new_hbm, sems.at[2])
    store.start()
    store.wait()


def beside(n, place, after, gradient, moment):
    rows, width = gradient.shape
    return call(
        functools.partial(beside_kernel, n),
        (shape((rows, CAP * n), BF), shape((rows, width), F32)),
        [VMEM, pl.BlockSpec(memory_space=pl.ANY), HBM, HBM],
        (VMEM, HBM),
        scratch=[
            pltpu.VMEM((rows, width), F32),
            pltpu.VMEM((rows, width), F32),
            pltpu.SemaphoreType.DMA((3,)),
        ],
        flops=4 * rows * width, nbytes=6 * 2**20,
    )(place, after, keep(gradient), keep(moment))


def unpack_kernel(n, back_hbm, order_ref, update_hbm, back_ref, scr, update_ref, sems):
    rows = update_ref.shape[0]
    part = CAP * n // PARTS
    loads = []
    for i in range(PARTS):
        chunk = pl.ds(2 * part * i, 2 * part)
        loads.append(pltpu.make_async_copy(back_hbm.at[chunk], back_ref.at[chunk], sems.at[i]))
        loads[i].start()
    halves = [pl.ds(i * (rows // 2), rows // 2) for i in range(2)]
    sums = [0.0, 0.0]
    for i in range(PARTS):
        chunk = pl.ds(2 * part * i, 2 * part)
        loads[i].wait()
        scr[chunk, :] = back_ref[chunk, :].astype(F32)
        came = column_halves(scr, part * i, part)
        for j, half in enumerate(halves):
            sums[j] = sums[j] + dot(order_ref[half, part * i : part * (i + 1)], came)
            if i == PARTS - 1:
                update_ref[half, :] = sums[j].astype(BF)
                store = pltpu.make_async_copy(update_ref.at[half], update_hbm.at[half], sems.at[PARTS + j])
                store.start()
                loads.append(store)
    for store in loads[PARTS:]:
        store.wait()


def unpack(n, back, order):
    rows = order.shape[0]
    return call(
        functools.partial(unpack_kernel, n),
        shape((rows, 2 * LANES), BF),
        [HBM, VMEM],
        HBM,
        scratch=[
            pltpu.VMEM((2 * CAP * n, LANES), BF),
            pltpu.VMEM((2 * CAP * n, LANES), F32),
            pltpu.VMEM((rows, 2 * LANES), BF),
            pltpu.SemaphoreType.DMA((PARTS + 2,)),
        ],
        flops=2 * CAP * n * rows * 2 * LANES, nbytes=2 * 2**20,
    )(keep(back), order)


def body(
    gradient, moment, left_stat, right_stat, left_root, right_root, seg_block, seg_row, owner_table
):
    n = lax.axis_size("dp")
    rows = gradient.shape[0]
    core = lax.axis_index("mp").astype(jnp.int32)
    swap = [(0, 1), (1, 0)]
    root_own = right_root[0]
    root_other = lax.ppermute(root_own, "mp", swap)

    send, place = pack(
        n, gradient, moment, seg_block[None, :], seg_row[None, :], owner_table[None, :]
    )
    send, root_other = lax.optimization_barrier((send, root_other))
    got = lax.all_to_all(send.reshape(n, OUT, 2, LANES), "dp", 0, 0, tiled=True)
    got = got.reshape(2 * OUT * n, LANES)
    tile_own, meta, root_near = tile(n, rows, got, root_own)
    tile_other = lax.ppermute(tile_own, "mp", swap)
    order, left_near = return_order(n, rows, meta, left_root[0])
    back = precond(
        n, core[None], tile_own, tile_other, order, root_near, root_other, left_near, left_root[0]
    )
    returned = lax.all_to_all(back.reshape(n, 2 * CAP, LANES), "dp", 0, 0, tiled=True)

    order, moment_new = beside(n, place, back, gradient, moment)
    tile_own, tile_other = tile_own[:rows], tile_other[:rows]
    whole = jnp.where(
        core == 0,
        jnp.concatenate([tile_own, tile_other], axis=1),
        jnp.concatenate([tile_other, tile_own], axis=1),
    )
    stat_rows = left_stat.shape[1]
    own_rows = lax.dynamic_slice_in_dim(whole, core * stat_rows, stat_rows, 0)
    left_new = GRAM_DECAY * left_stat[0] + dot_nt(own_rows, whole)
    right_new = GRAM_DECAY * right_stat[0] + lax.dot_general(
        tile_own, whole, (((0,), (0,)), ((), ())), preferred_element_type=F32
    )
    update = unpack(n, returned.reshape(2 * CAP * n, LANES), order)
    return (update, moment_new, left_new[None], right_new[None])


def solution(mesh):
    in_specs = (
        P("dp", "mp"),
        P("dp", "mp"),
        P("dp", "mp", None),
        P("dp", "mp", None),
        P("dp", None, None),
        P("dp", None, "mp"),
        P("dp"),
        P("dp"),
        P(),
    )
    out_specs = (P("dp", "mp"), P("dp", "mp"), P("dp", "mp", None), P("dp", "mp", None))
    return jax.shard_map(body, mesh=mesh, in_specs=in_specs, out_specs=out_specs, check_vma=False)
```

```python
import functools
import jax
import jax.numpy as jnp
from jax import lax
from jax.experimental import pallas as pl
from jax.experimental.pallas import tpu as pltpu
from jax.sharding import PartitionSpec as P

GRAM_DECAY = 0.95
MOMENT_DECAY = 0.99
ADAM_EPS = 1e-08
GRAFT_EPS = 1e-06

CAP = 12
OUT = CAP + 1
LANES = 128
BF = jnp.bfloat16
F32 = jnp.float32
VMEM_LIMIT = 32 * 1024 * 1024
EXTRA = 16
GROUP = 4
LOADS = 2
CHUNKS = 4
PARTS = 3
VMEM = pl.BlockSpec(memory_space=pltpu.VMEM)
SMEM = pl.BlockSpec(memory_space=pltpu.SMEM)
HBM = pl.BlockSpec(memory_space=pltpu.HBM)
shape = jax.ShapeDtypeStruct


def iota(shape, dim):
    return lax.broadcasted_iota(jnp.int32, shape, dim)


def dot(a, b):
    return jnp.dot(a, b, preferred_element_type=F32)


def dot_nt(a, b):
    return lax.dot_general(a, b, (((1,), (1,)), ((), ())), preferred_element_type=F32)


def onehot(mask):
    return jnp.where(mask, 1.0, 0.0).astype(BF)


def split3(x):
    hi = x.astype(BF)
    rest = x - hi.astype(F32)
    mid = rest.astype(BF)
    lo = (rest - mid.astype(F32)).astype(BF)
    return hi, mid, lo


def keep(x):
    return pltpu.with_memory_space_constraint(x, pltpu.HBM)


def call(kernel, out_shape, in_specs, out_specs=None, scratch=(), flops=0, nbytes=0):
    return pl.pallas_call(
        kernel,
        out_shape=out_shape,
        in_specs=in_specs,
        out_specs=out_specs if out_specs else jax.tree.map(lambda _: VMEM, out_shape),
        scratch_shapes=list(scratch),
        compiler_params=pltpu.CompilerParams(vmem_limit_bytes=VMEM_LIMIT),
        cost_estimate=pl.CostEstimate(flops=flops, bytes_accessed=nbytes, transcendentals=0),
    )


def ranks(dest):
    rows = dest.shape[1]
    step = 256 if rows % 256 == 0 else rows
    before = onehot(iota((step, step), 0) < iota((step, step), 1))
    found, parts = 0.0, []
    for start in range(0, rows, step):
        part = dest[:, start : start + step]
        parts.append(dot(part, before) + found)
        found = found + jnp.sum(part.astype(F32), axis=1, keepdims=True)
    return jnp.concatenate(parts, axis=1)


def next_moment(grad, moment):
    return MOMENT_DECAY * moment + (1.0 - MOMENT_DECAY) * (grad * grad)


def pack_kernel(
    n, grad_hbm, moment_hbm, block_hbm, row_hbm, owner_hbm, send_ref, place_ref, grad_ref,
    moment_ref, block_ref, row_ref, owner_ref, scr, sems,
):
    rows = grad_ref.shape[0]
    pairs = ((block_hbm, block_ref), (owner_hbm, owner_ref), (row_hbm, row_ref))
    copies = [pltpu.make_async_copy(a, b, sems.at[i]) for i, (a, b) in enumerate(pairs)]
    parts = [pl.ds(i * (rows // LOADS), rows // LOADS) for i in range(LOADS)]
    loads = [
        [
            pltpu.make_async_copy(grad_hbm.at[part], grad_ref.at[part], sems.at[3 + 2 * i]),
            pltpu.make_async_copy(moment_hbm.at[part], moment_ref.at[part], sems.at[4 + 2 * i]),
        ]
        for i, part in enumerate(parts)
    ]
    for copy in copies + sum(loads, []):
        copy.start()
    for copy in copies:
        copy.wait()
    block = block_ref[...]
    blocks = onehot(iota((n, rows), 0) == block)
    owner = jnp.broadcast_to(owner_ref[...], (16, n)).astype(F32).astype(BF)
    target = dot(owner, blocks)[0:1].astype(jnp.int32)
    mine = iota((n, rows), 0) == target
    dest = onehot(mine)
    slot = jnp.sum(jnp.where(mine, ranks(dest), 0.0), axis=0, keepdims=True).astype(jnp.int32)
    place_ref[...] = CAP * target + slot
    lane = iota((LANES, rows), 0)
    position = row_ref[...] + 1
    spread = jnp.where(lane == slot, position // 32, 0) + jnp.where(lane == slot + 16, position % 32, 0)
    meta = dot_nt(dest, spread.astype(F32).astype(BF))
    squares, coarse = [], []
    for part, (load_grad, load_moment) in zip(parts, loads):
        load_grad.wait()
        load_moment.wait()
        grad = grad_ref[part, :]
        coarse.append(grad.astype(BF))
        step = grad / (jnp.sqrt(next_moment(grad, moment_ref[part, :])) + ADAM_EPS)
        step_sq = step * step
        half = step_sq[:, :LANES] + step_sq[:, LANES:]
        squares.append(jnp.concatenate(split3(half), axis=1))
    coarse = jnp.concatenate(coarse, axis=0)
    for start in range(0, CAP, GROUP):
        slots = range(start, start + GROUP)
        order = jnp.concatenate([dest * onehot(slot == k) for k in slots], axis=0)
        placed = dot(order, coarse)
        for i, k in enumerate(slots):
            scr[pl.ds(2 * k, n, stride=2 * OUT), :] = placed[n * i : n * (i + 1), :LANES]
            scr[pl.ds(2 * k + 1, n, stride=2 * OUT), :] = placed[n * i : n * (i + 1), LANES:]
    adam = dot(dest, jnp.concatenate(squares, axis=0))
    a_hi, a_mid, a_lo = split3(jnp.sum(adam, axis=1, keepdims=True))
    col = iota((n, LANES), 1)
    meta = jnp.where(col == 32, a_hi.astype(F32), meta)
    meta = jnp.where(col == 33, a_mid.astype(F32), meta)
    meta = jnp.where(col == 34, a_lo.astype(F32), meta)
    scr[pl.ds(2 * CAP, n, stride=2 * OUT), :] = meta
    scr[pl.ds(2 * CAP + 1, n, stride=2 * OUT), :] = jnp.zeros((n, LANES), F32)
    send_ref[...] = scr[...].astype(BF)


def pack(n, gradient, moment, block, row, owner):
    rows, width = gradient.shape
    return call(
        functools.partial(pack_kernel, n),
        (shape((2 * OUT * n, LANES), BF), shape((1, rows), jnp.int32)),
        [HBM] * 5,
        scratch=[
            pltpu.VMEM((rows, width), F32),
            pltpu.VMEM((rows, width), F32),
            pltpu.VMEM((1, rows), jnp.int32),
            pltpu.VMEM((1, rows), jnp.int32),
            pltpu.VMEM((1, n), jnp.int32),
            pltpu.VMEM((2 * OUT * n, LANES), F32),
            pltpu.SemaphoreType.DMA((3 + 2 * LOADS,)),
        ],
        flops=2 * OUT * n * rows * width, nbytes=4 * 2**20,
    )(*[keep(x) for x in (gradient, moment, block, row, owner)])


def column_halves(scr, start, slots):
    left = scr[pl.ds(2 * start, slots, stride=2), :].astype(BF)
    right = scr[pl.ds(2 * start + 1, slots, stride=2), :].astype(BF)
    return jnp.concatenate([left, right], axis=1)


def tile_kernel(
    n, got_ref, root_hbm, tile_ref, meta_ref, root_ref, scr, sem
):
    load = pltpu.make_async_copy(root_hbm, root_ref, sem)
    load.start()
    rows = tile_ref.shape[0] - EXTRA
    scr[...] = got_ref[...].astype(F32)
    meta = scr[pl.ds(2 * CAP, n, stride=2 * OUT), :]
    meta_ref[...] = meta
    col = iota((n, LANES), 1)
    adam = jnp.sum(jnp.where((col >= 32) & (col < 35), meta, 0.0), axis=(0, 1), keepdims=True)
    col = iota((EXTRA, 2 * LANES), 1)
    extra = jnp.zeros((EXTRA, 2 * LANES), F32)
    for i, piece in enumerate(split3(adam)):
        extra = jnp.where(col == i, piece.astype(F32), extra)
    tile_ref[rows:, :] = extra.astype(BF)
    by_slot = meta.T
    position = (32.0 * by_slot[0:16] + by_slot[16:32]).astype(jnp.int32)
    came = []
    for k in range(CAP):
        left = scr[pl.ds(2 * k, n, stride=2 * OUT), :].astype(BF)
        right = scr[pl.ds(2 * k + 1, n, stride=2 * OUT), :].astype(BF)
        came.append(jnp.concatenate([left, right], axis=1))
    came = jnp.concatenate(came, axis=0)
    step = rows // 4
    for start in range(0, rows, step):
        row = iota((step, n), 0) + (start + 1)
        order = [onehot(row == position[k : k + 1]) for k in range(CAP)]
        tile_ref[start : start + step, :] = dot(jnp.concatenate(order, axis=1), came).astype(BF)
    load.wait()


def tile(n, rows, got, root):
    return call(
        functools.partial(tile_kernel, n),
        (
            shape((rows + EXTRA, 2 * LANES), BF), shape((n, LANES), F32), shape(root.shape, BF),
        ),
        [VMEM, HBM],
        scratch=[pltpu.VMEM((2 * OUT * n, LANES), F32), pltpu.SemaphoreType.DMA],
        flops=2 * OUT * n * rows * 2 * LANES, nbytes=3 * 2**20,
    )(got, keep(root))


def return_order_kernel(n, meta_ref, left_hbm, order_ref, left_ref, sem):
    load = pltpu.make_async_copy(left_hbm, left_ref, sem)
    load.start()
    rows = order_ref.shape[1]
    slots = iota((CAP * n, n), 0)
    source = iota((CAP * n, n), 1)
    expand = onehot((slots >= CAP * source) & (slots < CAP * source + CAP))
    meta = meta_ref[...]
    meta = jnp.where(iota((n, LANES), 1) < 16, 32.0 * meta, meta).astype(BF)
    by_slot = dot(expand, meta)
    which = iota((CAP * n, LANES), 0) % CAP
    lane = iota((CAP * n, LANES), 1)
    chosen = jnp.where((lane == which) | (lane == which + 16), by_slot, 0.0).astype(BF)
    position = dot(chosen, jnp.ones((LANES, LANES), BF)).astype(jnp.int32)
    lane = lane + 1
    for j in range(0, rows, LANES):
        order_ref[:, j : j + LANES] = onehot(position == lane + j)
    load.wait()


def return_order(n, rows, meta, left):
    return call(
        functools.partial(return_order_kernel, n),
        (shape((CAP * n, rows), BF), shape((rows, rows), BF)),
        [VMEM, HBM],
        scratch=[pltpu.SemaphoreType.DMA],
        flops=4 * CAP * n * n * LANES, nbytes=4 * 2**20,
    )(meta, keep(left))


def precond_kernel(
    n, core_ref, own_ref, other_ref, order_ref, root_own_ref, root_other_ref, left_ref,
    back_hbm, scr, back_ref, sems,
):
    rows, width = own_ref.shape[0] - EXTRA, own_ref.shape[1]
    quarter = rows // 4
    core = core_ref[0]
    own_rows = pl.ds(pl.multiple_of(core * width, width), width)
    other_rows = pl.ds(pl.multiple_of((1 - core) * width, width), width)
    both = jnp.concatenate([own_ref[:rows, :], other_ref[:rows, :]], axis=1)
    mixed = []
    for root_ref in (root_own_ref, root_other_ref):
        root = jnp.concatenate([root_ref[own_rows, :], root_ref[other_rows, :]], axis=0)
        mixed.append(dot(both, root).astype(BF))
    mixed_own, mixed_other = mixed
    parts, total = [], 0.0
    for i in range(4):
        left = left_ref[quarter * i : quarter * (i + 1), :]
        part, other_part = dot(left, mixed_own), dot(left, mixed_other)
        squares = part * part + other_part * other_part
        total = total + jnp.sum(squares.reshape(quarter // 8, 8, width), axis=0)
        parts.append(part)
    total = jnp.sum(total, axis=(0, 1), keepdims=True)
    extra = own_ref[rows:, :].astype(F32) + other_ref[rows:, :].astype(F32)
    adam = jnp.sum(extra[0:1], axis=(0, 1), keepdims=True)
    scale = jnp.sqrt(adam) / (jnp.sqrt(total) + GRAFT_EPS)
    grafted = jnp.concatenate([(part * scale).astype(BF) for part in parts], axis=0)
    part = CAP * n // CHUNKS
    stores = []
    for i in range(CHUNKS):
        chunk = pl.ds(2 * part * i, 2 * part)
        placed = dot(order_ref[part * i : part * (i + 1), :], grafted)
        scr[pl.ds(2 * part * i, part, stride=2), :] = placed[:, :LANES]
        scr[pl.ds(2 * part * i + 1, part, stride=2), :] = placed[:, LANES:]
        back_ref[chunk, :] = scr[chunk, :].astype(BF)
        store = pltpu.make_async_copy(back_ref.at[chunk], back_hbm.at[chunk], sems.at[i])
        store.start()
        stores.append(store)
    for store in stores:
        store.wait()


def precond(
    n, core, own, other, order, root_own, root_other, left
):
    rows, width = own.shape[0] - EXTRA, own.shape[1]
    return call(
        functools.partial(precond_kernel, n),
        shape((2 * CAP * n, LANES), BF),
        [SMEM] + [VMEM] * 6,
        HBM,
        scratch=[
            pltpu.VMEM((2 * CAP * n, LANES), F32),
            pltpu.VMEM((2 * CAP * n, LANES), BF),
            pltpu.SemaphoreType.DMA((CHUNKS,)),
        ],
        flops=8 * rows * rows * width, nbytes=5 * 2**20,
    )(core, own, other, order, root_own, root_other, left)


def beside_kernel(
    n, place_ref, after_ref, grad_hbm, moment_hbm, order_ref, new_hbm, grad_ref, moment_ref, sems
):
    del after_ref
    rows = order_ref.shape[0]
    loads = [
        pltpu.make_async_copy(grad_hbm, grad_ref, sems.at[0]),
        pltpu.make_async_copy(moment_hbm, moment_ref, sems.at[1]),
    ]
    for load in loads:
        load.start()
    place = jnp.broadcast_to(place_ref[...].astype(F32), (LANES, rows)).T.astype(jnp.int32)
    lane = iota((rows, LANES), 1)
    for j in range(0, CAP * n, LANES):
        order_ref[:, j : j + LANES] = onehot(place == lane + j)
    for load in loads:
        load.wait()
    moment_ref[...] = next_moment(grad_ref[...], moment_ref[...])
    store = pltpu.make_async_copy(moment_ref, new_hbm, sems.at[2])
    store.start()
    store.wait()


def beside(n, place, after, gradient, moment):
    rows, width = gradient.shape
    return call(
        functools.partial(beside_kernel, n),
        (shape((rows, CAP * n), BF), shape((rows, width), F32)),
        [VMEM, pl.BlockSpec(memory_space=pl.ANY), HBM, HBM],
        (VMEM, HBM),
        scratch=[
            pltpu.VMEM((rows, width), F32),
            pltpu.VMEM((rows, width), F32),
            pltpu.SemaphoreType.DMA((3,)),
        ],
        flops=4 * rows * width, nbytes=6 * 2**20,
    )(place, after, keep(gradient), keep(moment))


def unpack_kernel(n, back_hbm, order_ref, update_hbm, back_ref, scr, update_ref, sems):
    rows = update_ref.shape[0]
    part = CAP * n // PARTS
    loads = []
    for i in range(PARTS):
        chunk = pl.ds(2 * part * i, 2 * part)
        loads.append(pltpu.make_async_copy(back_hbm.at[chunk], back_ref.at[chunk], sems.at[i]))
        loads[i].start()
    halves = [pl.ds(i * (rows // 2), rows // 2) for i in range(2)]
    sums = [0.0, 0.0]
    for i in range(PARTS):
        chunk = pl.ds(2 * part * i, 2 * part)
        loads[i].wait()
        scr[chunk, :] = back_ref[chunk, :].astype(F32)
        came = column_halves(scr, part * i, part)
        for j, half in enumerate(halves):
            sums[j] = sums[j] + dot(order_ref[half, part * i : part * (i + 1)], came)
            if i == PARTS - 1:
                update_ref[half, :] = sums[j].astype(BF)
                store = pltpu.make_async_copy(update_ref.at[half], update_hbm.at[half], sems.at[PARTS + j])
                store.start()
                loads.append(store)
    for store in loads[PARTS:]:
        store.wait()


def unpack(n, back, order):
    rows = order.shape[0]
    return call(
        functools.partial(unpack_kernel, n),
        shape((rows, 2 * LANES), BF),
        [HBM, VMEM],
        HBM,
        scratch=[
            pltpu.VMEM((2 * CAP * n, LANES), BF),
            pltpu.VMEM((2 * CAP * n, LANES), F32),
            pltpu.VMEM((rows, 2 * LANES), BF),
            pltpu.SemaphoreType.DMA((PARTS + 2,)),
        ],
        flops=2 * CAP * n * rows * 2 * LANES, nbytes=2 * 2**20,
    )(keep(back), order)


def body(
    gradient, moment, left_stat, right_stat, left_root, right_root, seg_block, seg_row, owner_table
):
    n = lax.axis_size("dp")
    rows = gradient.shape[0]
    core = lax.axis_index("mp").astype(jnp.int32)
    swap = [(0, 1), (1, 0)]
    root_own = right_root[0]
    root_other = lax.ppermute(root_own, "mp", swap)

    send, place = pack(
        n, gradient, moment, seg_block[None, :], seg_row[None, :], owner_table[None, :]
    )
    send, root_other = lax.optimization_barrier((send, root_other))
    got = lax.all_to_all(send.reshape(n, OUT, 2, LANES), "dp", 0, 0, tiled=True)
    got = got.reshape(2 * OUT * n, LANES)
    tile_own, meta, root_near = tile(n, rows, got, root_own)
    tile_other = lax.ppermute(tile_own, "mp", swap)
    order, left = return_order(n, rows, meta, left_root[0])
    back = precond(
        n, core[None], tile_own, tile_other, order, root_near, root_other, left
    )
    returned = lax.all_to_all(back.reshape(n, 2 * CAP, LANES), "dp", 0, 0, tiled=True)

    order, moment_new = beside(n, place, back, gradient, moment)
    tile_own, tile_other = tile_own[:rows], tile_other[:rows]
    whole = jnp.where(
        core == 0,
        jnp.concatenate([tile_own, tile_other], axis=1),
        jnp.concatenate([tile_other, tile_own], axis=1),
    )
    stat_rows = left_stat.shape[1]
    own_rows = lax.dynamic_slice_in_dim(whole, core * stat_rows, stat_rows, 0)
    left_new = GRAM_DECAY * left_stat[0] + dot_nt(own_rows, whole)
    right_new = GRAM_DECAY * right_stat[0] + lax.dot_general(
        tile_own, whole, (((0,), (0,)), ((), ())), preferred_element_type=F32
    )
    update = unpack(n, returned.reshape(2 * CAP * n, LANES), order)
    return (update, moment_new, left_new[None], right_new[None])


def solution(mesh):
    in_specs = (
        P("dp", "mp"),
        P("dp", "mp"),
        P("dp", "mp", None),
        P("dp", "mp", None),
        P("dp", None, None),
        P("dp", None, "mp"),
        P("dp"),
        P("dp"),
        P(),
    )
    out_specs = (P("dp", "mp"), P("dp", "mp"), P("dp", "mp", None), P("dp", "mp", None))
    return jax.shard_map(body, mesh=mesh, in_specs=in_specs, out_specs=out_specs, check_vma=False)
```

```python
import functools
import jax
import jax.numpy as jnp
from jax import lax
from jax.experimental import pallas as pl
from jax.experimental.pallas import tpu as pltpu
from jax.sharding import PartitionSpec as P

GRAM_DECAY = 0.95
MOMENT_DECAY = 0.99
ADAM_EPS = 1e-08
GRAFT_EPS = 1e-06

CAP = 12
OUT = CAP + 1
LANES = 128
BF = jnp.bfloat16
F32 = jnp.float32
VMEM_LIMIT = 32 * 1024 * 1024
EXTRA = 16
GROUP = 4
LOADS = 2
CHUNKS = 4
PARTS = 3
STORES = 4
VMEM = pl.BlockSpec(memory_space=pltpu.VMEM)
SMEM = pl.BlockSpec(memory_space=pltpu.SMEM)
HBM = pl.BlockSpec(memory_space=pltpu.HBM)
shape = jax.ShapeDtypeStruct


def iota(shape, dim):
    return lax.broadcasted_iota(jnp.int32, shape, dim)


def dot(a, b):
    return jnp.dot(a, b, preferred_element_type=F32)


def dot_nt(a, b):
    return lax.dot_general(a, b, (((1,), (1,)), ((), ())), preferred_element_type=F32)


def onehot(mask):
    return jnp.where(mask, 1.0, 0.0).astype(BF)


def split3(x):
    hi = x.astype(BF)
    rest = x - hi.astype(F32)
    mid = rest.astype(BF)
    lo = (rest - mid.astype(F32)).astype(BF)
    return hi, mid, lo


def keep(x):
    return pltpu.with_memory_space_constraint(x, pltpu.HBM)


def call(kernel, out_shape, in_specs, out_specs=None, scratch=(), flops=0, nbytes=0):
    return pl.pallas_call(
        kernel,
        out_shape=out_shape,
        in_specs=in_specs,
        out_specs=out_specs if out_specs else jax.tree.map(lambda _: VMEM, out_shape),
        scratch_shapes=list(scratch),
        compiler_params=pltpu.CompilerParams(vmem_limit_bytes=VMEM_LIMIT),
        cost_estimate=pl.CostEstimate(flops=flops, bytes_accessed=nbytes, transcendentals=0),
    )


def ranks(dest):
    rows = dest.shape[1]
    step = 256 if rows % 256 == 0 else rows
    before = onehot(iota((step, step), 0) < iota((step, step), 1))
    found, parts = 0.0, []
    for start in range(0, rows, step):
        part = dest[:, start : start + step]
        parts.append(dot(part, before) + found)
        found = found + jnp.sum(part.astype(F32), axis=1, keepdims=True)
    return jnp.concatenate(parts, axis=1)


def next_moment(grad, moment):
    return MOMENT_DECAY * moment + (1.0 - MOMENT_DECAY) * (grad * grad)


def pack_kernel(
    n, grad_hbm, moment_hbm, block_hbm, row_hbm, owner_hbm, send_ref, place_ref, grad_ref,
    moment_ref, block_ref, row_ref, owner_ref, scr, sems,
):
    rows = grad_ref.shape[0]
    pairs = ((block_hbm, block_ref), (owner_hbm, owner_ref), (row_hbm, row_ref))
    copies = [pltpu.make_async_copy(a, b, sems.at[i]) for i, (a, b) in enumerate(pairs)]
    parts = [pl.ds(i * (rows // LOADS), rows // LOADS) for i in range(LOADS)]
    loads = [
        [
            pltpu.make_async_copy(grad_hbm.at[part], grad_ref.at[part], sems.at[3 + 2 * i]),
            pltpu.make_async_copy(moment_hbm.at[part], moment_ref.at[part], sems.at[4 + 2 * i]),
        ]
        for i, part in enumerate(parts)
    ]
    for copy in copies + sum(loads, []):
        copy.start()
    for copy in copies:
        copy.wait()
    block = block_ref[...]
    blocks = onehot(iota((n, rows), 0) == block)
    owner = jnp.broadcast_to(owner_ref[...], (16, n)).astype(F32).astype(BF)
    target = dot(owner, blocks)[0:1].astype(jnp.int32)
    mine = iota((n, rows), 0) == target
    dest = onehot(mine)
    slot = jnp.sum(jnp.where(mine, ranks(dest), 0.0), axis=0, keepdims=True).astype(jnp.int32)
    place_ref[...] = CAP * target + slot
    lane = iota((LANES, rows), 0)
    position = row_ref[...] + 1
    spread = jnp.where(lane == slot, position // 32, 0) + jnp.where(lane == slot + 16, position % 32, 0)
    meta = dot_nt(dest, spread.astype(F32).astype(BF))
    squares, coarse = [], []
    for part, (load_grad, load_moment) in zip(parts, loads):
        load_grad.wait()
        load_moment.wait()
        grad = grad_ref[part, :]
        coarse.append(grad.astype(BF))
        step = grad / (jnp.sqrt(next_moment(grad, moment_ref[part, :])) + ADAM_EPS)
        step_sq = step * step
        half = step_sq[:, :LANES] + step_sq[:, LANES:]
        squares.append(jnp.concatenate(split3(half), axis=1))
    coarse = jnp.concatenate(coarse, axis=0)
    for start in range(0, CAP, GROUP):
        slots = range(start, start + GROUP)
        order = jnp.concatenate([dest * onehot(slot == k) for k in slots], axis=0)
        placed = dot(order, coarse)
        for i, k in enumerate(slots):
            scr[pl.ds(2 * k, n, stride=2 * OUT), :] = placed[n * i : n * (i + 1), :LANES]
            scr[pl.ds(2 * k + 1, n, stride=2 * OUT), :] = placed[n * i : n * (i + 1), LANES:]
    adam = dot(dest, jnp.concatenate(squares, axis=0))
    a_hi, a_mid, a_lo = split3(jnp.sum(adam, axis=1, keepdims=True))
    col = iota((n, LANES), 1)
    meta = jnp.where(col == 32, a_hi.astype(F32), meta)
    meta = jnp.where(col == 33, a_mid.astype(F32), meta)
    meta = jnp.where(col == 34, a_lo.astype(F32), meta)
    scr[pl.ds(2 * CAP, n, stride=2 * OUT), :] = meta
    scr[pl.ds(2 * CAP + 1, n, stride=2 * OUT), :] = jnp.zeros((n, LANES), F32)
    send_ref[...] = scr[...].astype(BF)


def pack(n, gradient, moment, block, row, owner):
    rows, width = gradient.shape
    return call(
        functools.partial(pack_kernel, n),
        (shape((2 * OUT * n, LANES), BF), shape((1, rows), jnp.int32)),
        [HBM] * 5,
        scratch=[
            pltpu.VMEM((rows, width), F32),
            pltpu.VMEM((rows, width), F32),
            pltpu.VMEM((1, rows), jnp.int32),
            pltpu.VMEM((1, rows), jnp.int32),
            pltpu.VMEM((1, n), jnp.int32),
            pltpu.VMEM((2 * OUT * n, LANES), F32),
            pltpu.SemaphoreType.DMA((3 + 2 * LOADS,)),
        ],
        flops=2 * OUT * n * rows * width, nbytes=4 * 2**20,
    )(*[keep(x) for x in (gradient, moment, block, row, owner)])


def column_halves(scr, start, slots):
    left = scr[pl.ds(2 * start, slots, stride=2), :].astype(BF)
    right = scr[pl.ds(2 * start + 1, slots, stride=2), :].astype(BF)
    return jnp.concatenate([left, right], axis=1)


def tile_kernel(
    n, got_ref, root_hbm, tile_ref, meta_ref, root_ref, scr, sem
):
    load = pltpu.make_async_copy(root_hbm, root_ref, sem)
    load.start()
    rows = tile_ref.shape[0] - EXTRA
    scr[...] = got_ref[...].astype(F32)
    meta = scr[pl.ds(2 * CAP, n, stride=2 * OUT), :]
    meta_ref[...] = meta
    col = iota((n, LANES), 1)
    adam = jnp.sum(jnp.where((col >= 32) & (col < 35), meta, 0.0), axis=(0, 1), keepdims=True)
    col = iota((EXTRA, 2 * LANES), 1)
    extra = jnp.zeros((EXTRA, 2 * LANES), F32)
    for i, piece in enumerate(split3(adam)):
        extra = jnp.where(col == i, piece.astype(F32), extra)
    tile_ref[rows:, :] = extra.astype(BF)
    by_slot = meta.T
    position = (32.0 * by_slot[0:16] + by_slot[16:32]).astype(jnp.int32)
    came = []
    for k in range(CAP):
        left = scr[pl.ds(2 * k, n, stride=2 * OUT), :].astype(BF)
        right = scr[pl.ds(2 * k + 1, n, stride=2 * OUT), :].astype(BF)
        came.append(jnp.concatenate([left, right], axis=1))
    came = jnp.concatenate(came, axis=0)
    step = rows // 4
    for start in range(0, rows, step):
        row = iota((step, n), 0) + (start + 1)
        order = [onehot(row == position[k : k + 1]) for k in range(CAP)]
        tile_ref[start : start + step, :] = dot(jnp.concatenate(order, axis=1), came).astype(BF)
    load.wait()


def tile(n, rows, got, root):
    return call(
        functools.partial(tile_kernel, n),
        (
            shape((rows + EXTRA, 2 * LANES), BF), shape((n, LANES), F32), shape(root.shape, BF),
        ),
        [VMEM, HBM],
        scratch=[pltpu.VMEM((2 * OUT * n, LANES), F32), pltpu.SemaphoreType.DMA],
        flops=2 * OUT * n * rows * 2 * LANES, nbytes=3 * 2**20,
    )(got, keep(root))


def return_order_kernel(n, meta_ref, left_hbm, order_ref, left_ref, sem):
    load = pltpu.make_async_copy(left_hbm, left_ref, sem)
    load.start()
    rows = order_ref.shape[1]
    slots = iota((CAP * n, n), 0)
    source = iota((CAP * n, n), 1)
    expand = onehot((slots >= CAP * source) & (slots < CAP * source + CAP))
    meta = meta_ref[...]
    meta = jnp.where(iota((n, LANES), 1) < 16, 32.0 * meta, meta).astype(BF)
    by_slot = dot(expand, meta)
    which = iota((CAP * n, LANES), 0) % CAP
    lane = iota((CAP * n, LANES), 1)
    chosen = jnp.where((lane == which) | (lane == which + 16), by_slot, 0.0).astype(BF)
    position = dot(chosen, jnp.ones((LANES, LANES), BF)).astype(jnp.int32)
    lane = lane + 1
    for j in range(0, rows, LANES):
        order_ref[:, j : j + LANES] = onehot(position == lane + j)
    load.wait()


def return_order(n, rows, meta, left):
    return call(
        functools.partial(return_order_kernel, n),
        (shape((CAP * n, rows), BF), shape((rows, rows), BF)),
        [VMEM, HBM],
        scratch=[pltpu.SemaphoreType.DMA],
        flops=4 * CAP * n * n * LANES, nbytes=4 * 2**20,
    )(meta, keep(left))


def precond_kernel(
    n, core_ref, own_ref, other_ref, order_ref, root_own_ref, root_other_ref, left_ref,
    back_hbm, scr, back_ref, sems,
):
    rows, width = own_ref.shape[0] - EXTRA, own_ref.shape[1]
    quarter = rows // 4
    core = core_ref[0]
    own_rows = pl.ds(pl.multiple_of(core * width, width), width)
    other_rows = pl.ds(pl.multiple_of((1 - core) * width, width), width)
    both = jnp.concatenate([own_ref[:rows, :], other_ref[:rows, :]], axis=1)
    mixed = []
    for root_ref in (root_own_ref, root_other_ref):
        root = jnp.concatenate([root_ref[own_rows, :], root_ref[other_rows, :]], axis=0)
        mixed.append(dot(both, root).astype(BF))
    mixed_own, mixed_other = mixed
    parts, total = [], 0.0
    for i in range(4):
        left = left_ref[quarter * i : quarter * (i + 1), :]
        part, other_part = dot(left, mixed_own), dot(left, mixed_other)
        squares = part * part + other_part * other_part
        total = total + jnp.sum(squares.reshape(quarter // 8, 8, width), axis=0)
        parts.append(part)
    total = jnp.sum(total, axis=(0, 1), keepdims=True)
    extra = own_ref[rows:, :].astype(F32) + other_ref[rows:, :].astype(F32)
    adam = jnp.sum(extra[0:1], axis=(0, 1), keepdims=True)
    scale = jnp.sqrt(adam) / (jnp.sqrt(total) + GRAFT_EPS)
    grafted = jnp.concatenate([(part * scale).astype(BF) for part in parts], axis=0)
    part = CAP * n // CHUNKS
    stores = []
    for i in range(CHUNKS):
        chunk = pl.ds(2 * part * i, 2 * part)
        placed = dot(order_ref[part * i : part * (i + 1), :], grafted)
        scr[pl.ds(2 * part * i, part, stride=2), :] = placed[:, :LANES]
        scr[pl.ds(2 * part * i + 1, part, stride=2), :] = placed[:, LANES:]
        back_ref[chunk, :] = scr[chunk, :].astype(BF)
        store = pltpu.make_async_copy(back_ref.at[chunk], back_hbm.at[chunk], sems.at[i])
        store.start()
        stores.append(store)
    for store in stores:
        store.wait()


def precond(
    n, core, own, other, order, root_own, root_other, left
):
    rows, width = own.shape[0] - EXTRA, own.shape[1]
    return call(
        functools.partial(precond_kernel, n),
        shape((2 * CAP * n, LANES), BF),
        [SMEM] + [VMEM] * 6,
        HBM,
        scratch=[
            pltpu.VMEM((2 * CAP * n, LANES), F32),
            pltpu.VMEM((2 * CAP * n, LANES), BF),
            pltpu.SemaphoreType.DMA((CHUNKS,)),
        ],
        flops=8 * rows * rows * width, nbytes=5 * 2**20,
    )(core, own, other, order, root_own, root_other, left)


def beside_kernel(
    n, place_ref, after_ref, grad_hbm, moment_hbm, order_ref, new_hbm, grad_ref, moment_ref, sems
):
    del after_ref
    rows = order_ref.shape[0]
    loads = [
        pltpu.make_async_copy(grad_hbm, grad_ref, sems.at[0]),
        pltpu.make_async_copy(moment_hbm, moment_ref, sems.at[1]),
    ]
    for load in loads:
        load.start()
    place = jnp.broadcast_to(place_ref[...].astype(F32), (LANES, rows)).T.astype(jnp.int32)
    lane = iota((rows, LANES), 1)
    for j in range(0, CAP * n, LANES):
        order_ref[:, j : j + LANES] = onehot(place == lane + j)
    for load in loads:
        load.wait()
    moment_ref[...] = next_moment(grad_ref[...], moment_ref[...])
    store = pltpu.make_async_copy(moment_ref, new_hbm, sems.at[2])
    store.start()
    store.wait()


def beside(n, place, after, gradient, moment):
    rows, width = gradient.shape
    return call(
        functools.partial(beside_kernel, n),
        (shape((rows, CAP * n), BF), shape((rows, width), F32)),
        [VMEM, pl.BlockSpec(memory_space=pl.ANY), HBM, HBM],
        (VMEM, HBM),
        scratch=[
            pltpu.VMEM((rows, width), F32),
            pltpu.VMEM((rows, width), F32),
            pltpu.SemaphoreType.DMA((3,)),
        ],
        flops=4 * rows * width, nbytes=6 * 2**20,
    )(place, after, keep(gradient), keep(moment))


def unpack_kernel(n, back_hbm, order_ref, update_hbm, back_ref, scr, update_ref, sems):
    rows = update_ref.shape[0]
    part = CAP * n // PARTS
    loads = []
    for i in range(PARTS):
        chunk = pl.ds(2 * part * i, 2 * part)
        loads.append(pltpu.make_async_copy(back_hbm.at[chunk], back_ref.at[chunk], sems.at[i]))
        loads[i].start()
    groups = [pl.ds(i * (rows // STORES), rows // STORES) for i in range(STORES)]
    sums = [0.0] * STORES
    for i in range(PARTS):
        chunk = pl.ds(2 * part * i, 2 * part)
        loads[i].wait()
        scr[chunk, :] = back_ref[chunk, :].astype(F32)
        came = column_halves(scr, part * i, part)
        for j, group in enumerate(groups):
            sums[j] = sums[j] + dot(order_ref[group, part * i : part * (i + 1)], came)
            if i == PARTS - 1:
                update_ref[group, :] = sums[j].astype(BF)
                store = pltpu.make_async_copy(update_ref.at[group], update_hbm.at[group], sems.at[PARTS + j])
                store.start()
                loads.append(store)
    for store in loads[PARTS:]:
        store.wait()


def unpack(n, back, order):
    rows = order.shape[0]
    return call(
        functools.partial(unpack_kernel, n),
        shape((rows, 2 * LANES), BF),
        [HBM, VMEM],
        HBM,
        scratch=[
            pltpu.VMEM((2 * CAP * n, LANES), BF),
            pltpu.VMEM((2 * CAP * n, LANES), F32),
            pltpu.VMEM((rows, 2 * LANES), BF),
            pltpu.SemaphoreType.DMA((PARTS + STORES,)),
        ],
        flops=2 * CAP * n * rows * 2 * LANES, nbytes=2 * 2**20,
    )(keep(back), order)


def body(
    gradient, moment, left_stat, right_stat, left_root, right_root, seg_block, seg_row, owner_table
):
    n = lax.axis_size("dp")
    rows = gradient.shape[0]
    core = lax.axis_index("mp").astype(jnp.int32)
    swap = [(0, 1), (1, 0)]
    root_own = right_root[0]
    root_other = lax.ppermute(root_own, "mp", swap)

    send, place = pack(
        n, gradient, moment, seg_block[None, :], seg_row[None, :], owner_table[None, :]
    )
    send, root_other = lax.optimization_barrier((send, root_other))
    got = lax.all_to_all(send.reshape(n, OUT, 2, LANES), "dp", 0, 0, tiled=True)
    got = got.reshape(2 * OUT * n, LANES)
    tile_own, meta, root_near = tile(n, rows, got, root_own)
    tile_other = lax.ppermute(tile_own, "mp", swap)
    order, left = return_order(n, rows, meta, left_root[0])
    back = precond(
        n, core[None], tile_own, tile_other, order, root_near, root_other, left
    )
    returned = lax.all_to_all(back.reshape(n, 2 * CAP, LANES), "dp", 0, 0, tiled=True)

    order, moment_new = beside(n, place, back, gradient, moment)
    tile_own, tile_other = tile_own[:rows], tile_other[:rows]
    whole = jnp.where(
        core == 0,
        jnp.concatenate([tile_own, tile_other], axis=1),
        jnp.concatenate([tile_other, tile_own], axis=1),
    )
    stat_rows = left_stat.shape[1]
    own_rows = lax.dynamic_slice_in_dim(whole, core * stat_rows, stat_rows, 0)
    left_new = GRAM_DECAY * left_stat[0] + dot_nt(own_rows, whole)
    right_new = GRAM_DECAY * right_stat[0] + lax.dot_general(
        tile_own, whole, (((0,), (0,)), ((), ())), preferred_element_type=F32
    )
    update = unpack(n, returned.reshape(2 * CAP * n, LANES), order)
    return (update, moment_new, left_new[None], right_new[None])


def solution(mesh):
    in_specs = (
        P("dp", "mp"),
        P("dp", "mp"),
        P("dp", "mp", None),
        P("dp", "mp", None),
        P("dp", None, None),
        P("dp", None, "mp"),
        P("dp"),
        P("dp"),
        P(),
    )
    out_specs = (P("dp", "mp"), P("dp", "mp"), P("dp", "mp", None), P("dp", "mp", None))
    return jax.shard_map(body, mesh=mesh, in_specs=in_specs, out_specs=out_specs, check_vma=False)
```
